128 devices in a mesh: cuts: 8 (over y, core), shard: 16 (over z, x).
Axes of the slice: x: 4, y: 4, z: 4, core: 2. Of those that a mesh axis runs over, the one named last changes fastest.
Arguments:
- tokens: bfloat16 [512, 8192], P('cuts', 'shard'), may hold values from -6 to 6
- grad_out: bfloat16 [512, 8192], P('cuts', 'shard'), may hold values from -6 to 6
- counts: int32 [512], P('cuts'), may hold values from 1 to 8, as said below
- gate_weight: bfloat16 [28672, 8192], P(('cuts', 'shard')), may hold values from -0.0625 to 0.0625
- up_weight: bfloat16 [28672, 8192], P(('cuts', 'shard')), may hold values from -0.0625 to 0.0625
- down_weight: bfloat16 [28672, 8192], P(('cuts', 'shard')), may hold values from -0.03125 to 0.03125
Outputs:
- grad_in: bfloat16 [512, 8192], P('cuts', 'shard')
- grad_gate: bfloat16 [28672, 8192], P(('cuts', 'shard'))
- grad_up: bfloat16 [28672, 8192], P(('cuts', 'shard'))
- grad_down: bfloat16 [28672, 8192], P(('cuts', 'shard'))
The draws below stay inside these ranges and needn't reach their ends.
Inputs may be any that keep to these rules, and one draw needn't show every extreme that they name: `counts`: some token has 8 and some token has 1.
All inputs are finite; a program needn't handle non-finite values.
Results may differ from the reference program's by a relative error of at most 0.0049.
Values may be sent and summed in bfloat16 or wider, within the bound.
No kernel may reach another device: no remote copies, remote signals or barrier semaphores. Data moves between devices by JAX's collectives and lax.ppermute only.
A program may use at most 192 MiB of HBM per device.

```python
import jax
import jax.numpy as jnp

D = 8192
SLICE = 3584
FF = 28672
TOKENS = 512
N_CUTS = 8


def draw_counts(key, part):
    key = jax.random.fold_in(key, 11)
    first, second = jax.random.split(key)
    base = jax.random.randint(first, (TOKENS,), 1, N_CUTS + 1)
    spots = jax.random.randint(second, (2,), 0, TOKENS // 2)
    base = base.at[spots[0]].set(N_CUTS)
    base = base.at[TOKENS // 2 + spots[1]].set(1)
    return base.astype(jnp.int32)


def levels(rng, shape, pieces, least, high):
    def one(position, blocks):
        draws = jax.random.uniform(jax.random.fold_in(jax.random.fold_in(rng, 6), position), (blocks,), jnp.float32, least / len(pieces), high / len(pieces))
        return jnp.repeat(jnp.exp(draws), shape[position] // blocks).reshape((-1,) + (1,) * (len(shape) - position - 1))

    gain = one(*pieces[0])
    for cut in pieces[1:]:
        gain = gain * one(*cut)
    return gain


def scatter_about(stream_key, dims, deviation, limit, shards=(), dtype=jnp.bfloat16):
    result = jax.random.normal(stream_key, dims, jnp.float32) * deviation
    if len(shards) > 0:
        result = levels(stream_key, dims, shards, -0.22, 0.18) * result
    return jnp.clip(result, min=-limit, max=limit).astype(dtype)


def setup_inputs(seed: int = 0) -> dict:
    keys = jax.random.split(jax.random.key(seed), 7)
    tokens = scatter_about(keys[0], (TOKENS, D), 1.0, 6.0, ((0, 8), (1, 16)))
    grad_out = scatter_about(keys[1], (TOKENS, D), 1.0, 6.0, ((0, 8), (1, 16)))
    counts = draw_counts(jax.random.fold_in(keys[6], 71), 0)
    gate_weight = scatter_about(keys[3], (FF, D), D ** -0.5, 0.0625, ((0, 128),))
    up_weight = scatter_about(keys[4], (FF, D), D ** -0.5, 0.0625, ((0, 128),))
    down_weight = scatter_about(keys[5], (FF, D), FF ** -0.5, 0.03125, ((0, 128),))
    return dict(tokens=tokens, grad_out=grad_out, counts=counts, gate_weight=gate_weight, up_weight=up_weight, down_weight=down_weight)


def reference(tokens, grad_out, counts, gate_weight, up_weight, down_weight):
    grad_in = jnp.zeros(tokens.shape, jnp.float32)
    gate_parts = []
    up_parts = []
    down_parts = []
    for level in range(N_CUTS):
        low = level * SLICE
        w_gate = gate_weight[low:low + SLICE]
        w_up = up_weight[low:low + SLICE]
        w_down = down_weight[low:low + SLICE]
        keep = (counts > level).astype(jnp.float32)[:, None]
        gate = jnp.dot(tokens, w_gate.T, preferred_element_type=jnp.float32)
        upper = jnp.dot(tokens, w_up.T, preferred_element_type=jnp.float32)
        sigma = jax.nn.sigmoid(gate)
        hidden = (gate * sigma * upper * keep).astype(jnp.bfloat16)
        dhidden = jnp.dot(grad_out, w_down.T, preferred_element_type=jnp.float32) * keep
        dgate = (dhidden * upper * sigma * (1.0 + gate * (1.0 - sigma))).astype(jnp.bfloat16)
        dup = (dhidden * gate * sigma).astype(jnp.bfloat16)
        down_parts.append(jnp.dot(hidden.T, grad_out, preferred_element_type=jnp.float32).astype(jnp.bfloat16))
        gate_parts.append(jnp.dot(dgate.T, tokens, preferred_element_type=jnp.float32).astype(jnp.bfloat16))
        up_parts.append(jnp.dot(dup.T, tokens, preferred_element_type=jnp.float32).astype(jnp.bfloat16))
        grad_in = grad_in + jnp.dot(dgate, w_gate, preferred_element_type=jnp.float32)
        grad_in = grad_in + jnp.dot(dup, w_up, preferred_element_type=jnp.float32)
    return (grad_in.astype(jnp.bfloat16), jnp.concatenate(gate_parts, 0),
            jnp.concatenate(up_parts, 0), jnp.concatenate(down_parts, 0))
```

```python
import functools

import jax
import jax.numpy as jnp
from jax import lax
from jax.experimental import pallas as pl
from jax.experimental.pallas import tpu as pltpu
from jax.sharding import PartitionSpec as P

F32 = jnp.float32
BF16 = jnp.bfloat16
NT = (((1,), (1,)), ((), ()))
NN = (((1,), (0,)), ((), ()))
SIDE = 4
BLOCK = 512


def dot(a, b, dims):
    return lax.dot_general(a, b, dims, preferred_element_type=F32)


def moves(axis, step):
    if axis == "x":
        return "shard", [(z * 4 + x, z * 4 + (x + step) % 4) for z in range(4) for x in range(4)]
    if axis == "z":
        return "shard", [(z * 4 + x, (z + step) % 4 * 4 + x) for z in range(4) for x in range(4)]
    if axis == "y":
        return "cuts", [(y * 2 + c, (y + step) % 4 * 2 + c) for y in range(4) for c in range(2)]
    return "cuts", [(y * 2 + c, y * 2 + 1 - c) for y in range(4) for c in range(2)]


def shift(value, axis, step=1):
    name, pairs = moves(axis, step)
    return lax.ppermute(value, name, pairs)


def forward_kernel(rel, x_ref, g_ref, wg_ref, wu_ref, wd_ref, keep_ref, ht_ref, dgt_ref, dut_ref, dg_ref, du_ref, gate, up, dh, rows):
    step = pl.program_id(0)

    @pl.when(step == 0)
    def _():
        gate[...] = jnp.zeros_like(gate)
        up[...] = jnp.zeros_like(up)
        dh[...] = jnp.zeros_like(dh)

    for k in range(x_ref.shape[1]):
        cols = slice(k * BLOCK, (k + 1) * BLOCK)
        x = x_ref[:, k].reshape(512, BLOCK)
        g = g_ref[:, k].reshape(512, BLOCK)
        gate[...] += dot(wg_ref[:, cols], x, NT)
        up[...] += dot(wu_ref[:, cols], x, NT)
        dh[...] += dot(wd_ref[:, cols], g, NT)

    @pl.when(step == pl.num_programs(0) - 1)
    def _():
        keep = keep_ref[...]
        gv = gate[...]
        sig = 1.0 / (1.0 + jnp.exp(-gv))
        silu = gv * sig
        dhv = dh[...] * keep
        uv = up[...]
        ht_ref[...] = (silu * uv * keep).astype(BF16)
        dg = dhv * uv * sig * (1.0 + gv * (1.0 - sig))
        du = dhv * silu
        dgt_ref[...] = dg.astype(BF16)
        dut_ref[...] = du.astype(BF16)
        for value, out in ((dg, dg_ref), (du, du_ref)):
            rows[...] = value.T.astype(BF16).reshape(8, 64, 224)
            for r in range(8):
                out[r // 4, :, r % 4] = rows[rel[r]].reshape(2, 32, 224)


def forward(rel, both, wg, wu, wd, keep):
    width = 1024
    per = width // BLOCK
    wspec = pl.BlockSpec((224, width), lambda s, rel: (0, s))
    tspec = pl.BlockSpec((224, 512), lambda s, rel: (0, 0))
    dspec = pl.BlockSpec((2, 2, 4, 32, 224), lambda s, rel: (0, 0, 0, 0, 0))
    return pl.pallas_call(
        forward_kernel,
        grid_spec=pltpu.PrefetchScalarGridSpec(
            num_scalar_prefetch=1,
            grid=(8192 // width,),
            in_specs=[
                pl.BlockSpec((8, per, 64, BLOCK), lambda s, rel: (0, s, 0, 0)),
                pl.BlockSpec((8, per, 64, BLOCK), lambda s, rel: (0, s, 1, 0)),
                wspec, wspec, wspec,
                pl.BlockSpec((1, 512), lambda s, rel: (0, 0)),
            ],
            out_specs=[tspec, tspec, tspec, dspec, dspec],
            scratch_shapes=[pltpu.VMEM((224, 512), F32)] * 3 + [pltpu.VMEM((8, 64, 224), BF16)],
        ),
        out_shape=[jax.ShapeDtypeStruct((224, 512), BF16)] * 3
        + [jax.ShapeDtypeStruct((2, 2, 4, 32, 224), BF16)] * 2,
        compiler_params=pltpu.CompilerParams(vmem_limit_bytes=48 * 2**20),
        cost_estimate=pl.CostEstimate(flops=6 * 512 * 224 * 8192, bytes_accessed=28 * 2**20, transcendentals=512 * 224),
    )(rel, both, both, wg, wu, wd, keep)


def weight_grad_kernel(x_ref, g_ref, ht_ref, dgt_ref, dut_ref, gg_ref, gu_ref, gd_ref):
    for k in range(x_ref.shape[1]):
        cols = slice(k * BLOCK, (k + 1) * BLOCK)
        x = x_ref[:, k].reshape(512, BLOCK)
        g = g_ref[:, k].reshape(512, BLOCK)
        gg_ref[:, cols] = dot(dgt_ref[...], x, NN).astype(BF16)
        gu_ref[:, cols] = dot(dut_ref[...], x, NN).astype(BF16)
        gd_ref[:, cols] = dot(ht_ref[...], g, NN).astype(BF16)


def weight_grads(both, ht, dgt, dut):
    width = 1024
    per = width // BLOCK
    wspec = pl.BlockSpec((224, width), lambda s: (0, s))
    tspec = pl.BlockSpec((224, 512), lambda s: (0, 0))
    return pl.pallas_call(
        weight_grad_kernel,
        grid=(8192 // width,),
        in_specs=[
            pl.BlockSpec((8, per, 64, BLOCK), lambda s: (0, s, 0, 0)),
            pl.BlockSpec((8, per, 64, BLOCK), lambda s: (0, s, 1, 0)),
            tspec, tspec, tspec,
        ],
        out_specs=[wspec] * 3,
        out_shape=[jax.ShapeDtypeStruct((224, 8192), BF16)] * 3,
        compiler_params=pltpu.CompilerParams(vmem_limit_bytes=48 * 2**20),
        cost_estimate=pl.CostEstimate(flops=6 * 512 * 224 * 8192, bytes_accessed=28 * 2**20, transcendentals=0),
    )(both, both, ht, dgt, dut)


def partner_kernel(tab, dg_ref, du_ref, wg_ref, wu_ref, p_ref, q_ref):
    dg = dg_ref[0].reshape(256, 224)
    du = du_ref[0].reshape(256, 224)
    for dx in range(SIDE):
        cols = pl.ds(pl.multiple_of(tab[4 + dx] * BLOCK, BLOCK), BLOCK)
        total = dot(dg, wg_ref[:, cols], NN) + dot(du, wu_ref[:, cols], NN)
        p_ref[dx, 0] = total[:128].astype(BF16)
        q_ref[0, dx] = total[128:].astype(BF16)


def partner_terms(tab, dg, du, wg, wu):
    dspec = pl.BlockSpec((1, 2, 4, 32, 224), lambda dz, tab: (1, 0, 0, 0, 0))
    wspec = pl.BlockSpec((224, 4 * BLOCK), lambda dz, tab: (0, tab[dz]))
    return pl.pallas_call(
        partner_kernel,
        grid_spec=pltpu.PrefetchScalarGridSpec(
            num_scalar_prefetch=1,
            grid=(SIDE,),
            in_specs=[dspec, dspec, wspec, wspec],
            out_specs=[
                pl.BlockSpec((4, 1, 128, BLOCK), lambda dz, tab: (0, dz, 0, 0)),
                pl.BlockSpec((1, 4, 128, BLOCK), lambda dz, tab: (dz, 0, 0, 0)),
            ],
        ),
        out_shape=[jax.ShapeDtypeStruct((4, 4, 128, BLOCK), BF16)] * 2,
        compiler_params=pltpu.CompilerParams(vmem_limit_bytes=48 * 2**20),
        cost_estimate=pl.CostEstimate(flops=4 * 256 * 224 * 8192, bytes_accessed=12 * 2**20, transcendentals=0),
    )(tab, dg, du, wg, wu)


def own_kernel(by_x, tab, dg_ref, du_ref, wg_ref, wu_ref, add_ref, *outs):
    dz = pl.program_id(0)
    dg = dg_ref[0].reshape(128, 224)
    du = du_ref[0].reshape(128, 224)
    for dx in range(SIDE):
        cols = pl.ds(pl.multiple_of(tab[4 + dx] * BLOCK, BLOCK), BLOCK)
        total = dot(dg, wg_ref[:, cols], NN) + dot(du, wu_ref[:, cols], NN)
        if by_x:
            outs[dx][0] = (total + add_ref[dx, 0].astype(F32)).astype(BF16)
        else:
            done = (total + add_ref[0, dx].astype(F32)).astype(BF16)
            for k in range(SIDE):
                @pl.when(dz == k)
                def _(k=k, done=done, dx=dx):
                    outs[k][dx] = done


def own_terms(by_x, tab, dg, du, wg, wu, add):
    half = 0 if by_x else 1
    dspec = pl.BlockSpec((1, 1, 4, 32, 224), lambda dz, tab: (0, half, 0, 0, 0))
    wspec = pl.BlockSpec((224, 4 * BLOCK), lambda dz, tab: (0, tab[dz]))
    if by_x:
        aspec = pl.BlockSpec((4, 1, 128, BLOCK), lambda dz, tab: (0, dz, 0, 0))
        ospec = pl.BlockSpec((1, 128, BLOCK), lambda dz, tab: (dz, 0, 0))
    else:
        aspec = pl.BlockSpec((1, 4, 128, BLOCK), lambda dz, tab: (dz, 0, 0, 0))
        ospec = pl.BlockSpec((4, 128, BLOCK), lambda dz, tab: (0, 0, 0))
    return pl.pallas_call(
        functools.partial(own_kernel, by_x),
        grid_spec=pltpu.PrefetchScalarGridSpec(
            num_scalar_prefetch=1,
            grid=(SIDE,),
            in_specs=[dspec, dspec, wspec, wspec, aspec],
            out_specs=[ospec] * 4,
        ),
        out_shape=[jax.ShapeDtypeStruct((4, 128, BLOCK), BF16)] * 4,
        compiler_params=pltpu.CompilerParams(vmem_limit_bytes=48 * 2**20),
        cost_estimate=pl.CostEstimate(flops=4 * 128 * 224 * 8192, bytes_accessed=12 * 2**20, transcendentals=0),
    )(tab, dg, du, wg, wu, add)


def sum_kernel(a, b, c, d, *outs):
    for k in range(SIDE):
        outs[k][...] = (
            (a[k].astype(F32) + b[k].astype(F32)) + (c[k].astype(F32) + d[k].astype(F32))
        ).astype(BF16)


def sum_apart(parts):
    return pl.pallas_call(
        sum_kernel,
        out_shape=[jax.ShapeDtypeStruct((128, BLOCK), BF16)] * 4,
        cost_estimate=pl.CostEstimate(flops=3 * 4 * 128 * 512, bytes_accessed=5 * 2**19, transcendentals=0),
    )(*parts)


def join_kernel(*refs):
    ins, outs = refs[:8], refs[8:]
    for h in range(2):
        total = (ins[4 * h][...].astype(F32) + ins[4 * h + 1][...].astype(F32)) + (
            ins[4 * h + 2][...].astype(F32) + ins[4 * h + 3][...].astype(F32)
        )
        for k in range(SIDE):
            outs[k][h * 32:(h + 1) * 32] = total[k * 32:(k + 1) * 32].astype(BF16)


def join_apart(first, second):
    return pl.pallas_call(
        join_kernel,
        out_shape=[jax.ShapeDtypeStruct((64, BLOCK), BF16)] * 4,
        cost_estimate=pl.CostEstimate(flops=2**19, bytes_accessed=5 * 2**18, transcendentals=0),
    )(*first, *second)


def exchange(pieces, axis):
    return [pieces[0]] + [shift(pieces[d], axis, d) for d in (1, 3, 2)]


def body(tokens, grad_out, counts, gate_weight, up_weight, down_weight):
    c = lax.axis_index("cuts")
    s = lax.axis_index("shard")
    y, core, z, x = c // 2, c % 2, s // 4, s % 4
    step = jnp.arange(SIDE, dtype=jnp.int32)
    near = (y + step) % 4 * 2
    rel = jnp.concatenate([near + core, near + 1 - core]).astype(jnp.int32)
    tab = jnp.concatenate([(z + step) % 4, (x + step) % 4]).astype(jnp.int32)

    both = lax.all_gather(jnp.concatenate([tokens, grad_out], 0), ("cuts", "shard"), tiled=False)
    both = both.reshape(8, 16, 128, BLOCK)
    all_counts = lax.all_gather(counts, "cuts", tiled=True)
    keep = (all_counts > c).astype(F32).reshape(1, 512)

    ht, dgt, dut, dg, du = forward(rel, both, gate_weight, up_weight, down_weight, keep)
    first, second = partner_terms(tab, dg, du, gate_weight, up_weight)
    first, second = shift(first, "core"), shift(second, "core")
    first = own_terms(True, tab, dg, du, gate_weight, up_weight, first)
    second = own_terms(False, tab, dg, du, gate_weight, up_weight, second)
    first = exchange(first, "x")
    second = exchange(second, "z")
    grad_gate, grad_up, grad_down = weight_grads(both, ht, dgt, dut)
    first = exchange(sum_apart(first), "z")
    second = exchange(sum_apart(second), "x")
    parts = exchange(join_apart(first, second), "y")
    total = (parts[0].astype(F32) + parts[1].astype(F32)) + (parts[2].astype(F32) + parts[3].astype(F32))
    return (total.astype(BF16), grad_gate, grad_up, grad_down)


def solution(mesh):
    return jax.shard_map(
        body,
        mesh=mesh,
        in_specs=(
            P("cuts", "shard"),
            P("cuts", "shard"),
            P("cuts"),
            P(("cuts", "shard"), None),
            P(("cuts", "shard"), None),
            P(("cuts", "shard"), None),
        ),
        out_specs=(
            P("cuts", "shard"),
            P(("cuts", "shard"), None),
            P(("cuts", "shard"), None),
            P(("cuts", "shard"), None),
        ),
        check_vma=False,
    )
```

```python
import functools

import jax
import jax.numpy as jnp
from jax import lax
from jax.experimental import pallas as pl
from jax.experimental.pallas import tpu as pltpu
from jax.sharding import PartitionSpec as P

F32 = jnp.float32
BF16 = jnp.bfloat16
NT = (((1,), (1,)), ((), ()))
NN = (((1,), (0,)), ((), ()))
SIDE = 4
wait = lax.optimization_barrier
BLOCK = 512
MIB = 2**20


def dot(a, b, dims):
    return lax.dot_general(a, b, dims, preferred_element_type=F32)


def moves(axis, step):
    if axis == "x":
        return "shard", [(z * 4 + x, z * 4 + (x + step) % 4) for z in range(4) for x in range(4)]
    if axis == "z":
        return "shard", [(z * 4 + x, (z + step) % 4 * 4 + x) for z in range(4) for x in range(4)]
    if axis == "y":
        return "cuts", [(y * 2 + c, (y + step) % 4 * 2 + c) for y in range(4) for c in range(2)]
    return "cuts", [(y * 2 + c, y * 2 + 1 - c) for y in range(4) for c in range(2)]


def across(first, third, core, axis):
    pairs = []
    for y in range(4):
        for c in range(2):
            for z in range(4):
                for x in range(4):
                    step = -1 if c == 0 else 1
                    to_z, to_x = (z, (x + step) % 4) if axis == "x" else ((z + step) % 4, x)
                    pairs.append(((y * 2 + c) * 16 + z * 4 + x, (y * 2 + c) * 16 + to_z * 4 + to_x))
    return lax.ppermute(jnp.where(core == 0, first, third), ("cuts", "shard"), pairs)


def shift(value, axis, step=1):
    name, pairs = moves(axis, step)
    return lax.ppermute(value, name, pairs)


VMEM = pl.BlockSpec(memory_space=pltpu.VMEM)
ANY = pl.BlockSpec(memory_space=pl.ANY)
SMEM = pl.BlockSpec(memory_space=pltpu.SMEM)


def lanes(tab, at):
    return pl.ds(pl.multiple_of(tab[at] * BLOCK, BLOCK), BLOCK)


def wide(tab, at):
    return pl.ds(pl.multiple_of(tab[at] * 4 * BLOCK, 4 * BLOCK), 4 * BLOCK)


def sigmoid(v):
    return 1.0 / (1.0 + jnp.exp(-v))


def forward_kernel(es, first, last, tab, wg, wu, wd, *refs):
    refs, (bg, bu, bd, sems) = refs[:-4], refs[-4:]
    pieces, refs = refs[:4 * len(es)], refs[4 * len(es):]
    before = () if first else refs[:3]
    refs = refs[len(before):]
    keep_ref = refs[0] if last else None
    outs = refs[1:] if last else refs
    copies = []
    for n, e in enumerate(es):
        cols = wide(tab, 32 + e)
        copies += [
            [pltpu.make_async_copy(wg.at[:, cols], bg.at[n], sems.at[n, 0])],
            [pltpu.make_async_copy(wu.at[:, cols], bu.at[n], sems.at[n, 1])],
            [
                pltpu.make_async_copy(wd.at[:, lanes(tab, 16 + 4 * e + d)], bd.at[n, d], sems.at[n, 2 + d])
                for d in range(SIDE)
            ],
        ]
    for group in copies:
        for copy in group:
            copy.start()
    sums = ([], [], [])
    for n in range(len(es)):
        for m in range(3):
            data = pieces[4 * n + 2 * (m // 2):4 * n + 2 * (m // 2) + 2]
            for copy in copies[3 * n + m]:
                copy.wait()
            for side in range(2):
                cols = slice(side * 256, side * 256 + 256)
                total = outs[m][:, cols] if n else None if first else before[m][:, cols]
                for d in range(SIDE):
                    w = bd[n, d] if m == 2 else (bg, bu)[m][n, :, lanes(tab, 36 + d)]
                    term = dot(w, data[side][d], NT)
                    total = term if total is None else total + term
                if last:
                    sums[m].append(total)
                else:
                    outs[m][:, cols] = total
    if last:
        ht_ref, dgt_ref, dut_ref, own_ref, far_ref = outs
        for side, out in ((1, far_ref), (0, own_ref)):
            cols = slice(side * 256, side * 256 + 256)
            keep = keep_ref[:, cols]
            gv, uv, dhv = sums[0][side], sums[1][side], sums[2][side] * keep
            sig = sigmoid(gv)
            silu = gv * sig
            ht_ref[:, cols] = (silu * uv * keep).astype(BF16)
            dg = dhv * uv * sig * (1.0 + gv * (1.0 - sig))
            du = dhv * silu
            dgt_ref[:, cols] = dg.astype(BF16)
            dut_ref[:, cols] = du.astype(BF16)
            for k, value in enumerate((dg, du)):
                turned = value.T.astype(BF16)
                for b in range(SIDE):
                    for half in range(2):
                        low = b * 64 + half * 32
                        out[k, half, b * 32:b * 32 + 32] = turned[low:low + 32]


def forward(es, tab, weights, pieces, before, keep):
    first, last, count = not before, keep is not None, len(es)
    operands = [tab, *weights, *pieces, *before]
    if last:
        operands.append(keep)
        out_shape = [jax.ShapeDtypeStruct((224, 512), BF16)] * 3 + [jax.ShapeDtypeStruct((2, 2, 128, 224), BF16)] * 2
    else:
        out_shape = [jax.ShapeDtypeStruct((224, 512), F32)] * 3
    return pl.pallas_call(
        functools.partial(forward_kernel, es, first, last),
        in_specs=[SMEM] + [ANY] * 3 + [VMEM] * (len(operands) - 4),
        out_specs=[VMEM] * len(out_shape),
        out_shape=out_shape,
        scratch_shapes=[
            pltpu.VMEM((count, 224, 4 * BLOCK), BF16),
            pltpu.VMEM((count, 224, 4 * BLOCK), BF16),
            pltpu.VMEM((count, 4, 224, BLOCK), BF16),
            pltpu.SemaphoreType.DMA((count, 6)),
        ],
        compiler_params=pltpu.CompilerParams(vmem_limit_bytes=(6 + 7 * count) * MIB),
        cost_estimate=pl.CostEstimate(flops=count * 6 * 512 * 224 * 2048, bytes_accessed=count * 8 * MIB, transcendentals=0),
    )(*operands)


def token_grad_kernel(tab, dgt_ref, dut_ref, *refs):
    pieces, outs = refs[:8], refs[8:]
    for e in range(SIDE):
        @pl.when(pl.program_id(0) == e)
        def _(e=e):
            for d in range(SIDE):
                x0, x1 = pieces[2 * e][d], pieces[2 * e + 1][d]
                for row, out in zip((dgt_ref, dut_ref), outs):
                    out[:, lanes(tab, 36 + d)] = (dot(row[:, :256], x0, NN) + dot(row[:, 256:], x1, NN)).astype(BF16)


def down_grad_kernel(tab, ht_ref, *refs):
    pieces, out = refs[:8], refs[8]
    d = pl.program_id(0)
    for e in range(SIDE):
        g0, g1 = pieces[2 * e][d], pieces[2 * e + 1][d]
        out[:, lanes(tab, 36 + e)] = (dot(ht_ref[:, :256], g0, NN) + dot(ht_ref[:, 256:], g1, NN)).astype(BF16)


def weight_grads(kernel, tab, rows, own, far):
    pieces = [p for e in range(SIDE) for p in (own[e], far[e])]
    count = len(rows)
    return pl.pallas_call(
        kernel,
        grid_spec=pltpu.PrefetchScalarGridSpec(
            num_scalar_prefetch=1,
            grid=(SIDE,),
            in_specs=[VMEM] * (count + len(pieces)),
            out_specs=[pl.BlockSpec((224, 4 * BLOCK), lambda k, tab: (0, tab[32 + k]))] * count,
        ),
        out_shape=[jax.ShapeDtypeStruct((224, 8192), BF16)] * count,
        compiler_params=pltpu.CompilerParams(vmem_limit_bytes=14 * MIB),
        cost_estimate=pl.CostEstimate(flops=count * 2 * 512 * 224 * 8192, bytes_accessed=count * 6 * MIB, transcendentals=0),
    )(tab, *rows, *pieces)


def input_grad_kernel(tab, own_ref, far_ref, *refs):
    weights, outs, (held, sems) = refs[:4], refs[4:12], refs[12:]
    rows = [ref[k].reshape(256, 224) for ref in (own_ref, far_ref) for k in range(2)]

    def fetch(dz):
        return [
            pltpu.make_async_copy(w.at[:, wide(tab, 32 + dz)], held.at[dz % 2, n], sems.at[dz % 2, n])
            for n, w in enumerate(weights)
        ]

    copies = fetch(0)
    for copy in copies:
        copy.start()
    for dz in range(SIDE):
        current = copies
        if dz < SIDE - 1:
            copies = fetch(dz + 1)
            for copy in copies:
                copy.start()
        for copy in current:
            copy.wait()
        for dx in range(SIDE):
            cols = lanes(tab, 36 + dx)
            w = [held[dz % 2, n, :, cols] for n in range(4)]
            total = (dot(rows[0], w[0], NN) + dot(rows[1], w[1], NN)) + (dot(rows[2], w[2], NN) + dot(rows[3], w[3], NN))
            done = total.astype(BF16)
            outs[dx][dz] = done[:128]
            outs[4 + dz][dx] = done[128:]


def input_grads(tab, own, far, weights):
    return pl.pallas_call(
        input_grad_kernel,
        in_specs=[SMEM] + [VMEM] * 2 + [ANY] * 4,
        out_specs=[VMEM] * 8,
        out_shape=[jax.ShapeDtypeStruct((4, 128, BLOCK), BF16)] * 8,
        scratch_shapes=[pltpu.VMEM((2, 4, 224, 4 * BLOCK), BF16), pltpu.SemaphoreType.DMA((2, 4))],
        compiler_params=pltpu.CompilerParams(vmem_limit_bytes=16 * MIB),
        cost_estimate=pl.CostEstimate(flops=8 * 256 * 224 * 8192, bytes_accessed=18 * MIB, transcendentals=0),
    )(tab, own, far, *weights)


def sum_kernel(a, b, c, d, *outs):
    for k in range(SIDE):
        outs[k][...] = (
            (a[k].astype(F32) + b[k].astype(F32)) + (c[k].astype(F32) + d[k].astype(F32))
        ).astype(BF16)


def sum_apart(parts):
    return pl.pallas_call(
        sum_kernel,
        out_shape=[jax.ShapeDtypeStruct((128, BLOCK), BF16)] * 4,
        compiler_params=pltpu.CompilerParams(vmem_limit_bytes=4 * MIB),
        cost_estimate=pl.CostEstimate(flops=3 * 4 * 128 * 512, bytes_accessed=5 * 2**19, transcendentals=0),
    )(*parts)


def join_kernel(*refs):
    ins, outs = refs[:8], refs[8:]
    for h in range(2):
        total = (ins[4 * h][...].astype(F32) + ins[4 * h + 1][...].astype(F32)) + (
            ins[4 * h + 2][...].astype(F32) + ins[4 * h + 3][...].astype(F32)
        )
        for k in range(SIDE):
            outs[k][h * 32:(h + 1) * 32] = total[k * 32:(k + 1) * 32].astype(BF16)


def join_apart(first, second):
    return pl.pallas_call(
        join_kernel,
        out_shape=[jax.ShapeDtypeStruct((64, BLOCK), BF16)] * 4,
        compiler_params=pltpu.CompilerParams(vmem_limit_bytes=4 * MIB),
        cost_estimate=pl.CostEstimate(flops=2**19, bytes_accessed=5 * 2**18, transcendentals=0),
    )(*first, *second)


def exchange(pieces, axis):
    return [pieces[0]] + [shift(pieces[d], axis, d) for d in (1, 3, 2)]


def exchange_in_two(first, second, fill):
    near = [shift(p[d], axis, d) for p, axis in (first, second) for d in (1, 3)]
    near, done0 = wait((near, fill[0]()))
    ends = [first[0][2], second[0][2]]
    ends, near = wait((ends, near))
    ends = [shift(ends[0], first[1], 2), shift(ends[1], second[1], 2)]
    ends, done1 = wait((ends, fill[1]()))
    return [first[0][0], *near[:2], ends[0]], [second[0][0], *near[2:], ends[1]], done0, done1


def around(value, axis):
    return [value] + [shift(value, axis, -e % SIDE) for e in (1, 2, 3)]


def body(tokens, grad_out, counts, gate_weight, up_weight, down_weight):
    c = lax.axis_index("cuts")
    s = lax.axis_index("shard")
    core, z, x = c % 2, s // 4, s % 4
    step = jnp.arange(SIDE, dtype=jnp.int32)
    zs, xs = (z + step) % 4, (x + step) % 4
    by_z = zs[:, None] * 4 + xs[None, :]
    tab = jnp.concatenate([by_z.reshape(16), by_z.T.reshape(16), zs, xs]).astype(jnp.int32)
    weights = (gate_weight, up_weight, down_weight)

    row = jnp.pad(counts.astype(BF16)[None, :], ((0, 15), (0, BLOCK - 64)))
    blocks = around(jnp.concatenate([tokens, grad_out, row], 0), "y")
    blocks, far_gate, far_up = wait((blocks, shift(gate_weight, "core"), shift(up_weight, "core")))

    x0 = jnp.concatenate([b[:64] for b in blocks], 0)
    g0 = jnp.concatenate([b[64:128] for b in blocks], 0)
    own_counts = jnp.concatenate([b[128:129, :64] for b in blocks], 1)
    ahead = shift(x0, "x", 3)
    held, ahead = wait((g0, ahead))
    x0 = [x0, ahead, shift(x0, "x", 2), shift(x0, "x", 1)]
    g0 = [g0, shift(g0, "z", 3), shift(g0, "z", 2), shift(held, "z", 1)]
    x0, g0 = wait((x0, g0))
    x0, g0 = jnp.stack(x0), jnp.stack(g0)

    own_x, own_g, far_x, far_g = {0: x0}, {0: g0}, {}, {}

    def swap(e):
        far_x[e], far_g[e] = shift(own_x[e], "core"), shift(own_g[e], "core")

    def add(es, before, keep=None):
        pieces = [p[e] for e in es for p in (own_x, far_x, own_g, far_g)]
        return forward(es, tab, weights, pieces, before, keep)

    near = [shift(x0, "z", 3), shift(x0, "z", 1), shift(g0, "x", 3), shift(g0, "x", 1)]
    swap(0)
    all_counts = jnp.concatenate([own_counts, shift(own_counts, "core")], 1)
    keep = (all_counts.astype(F32) > c.astype(F32)).astype(F32)
    sums = add((0,), ())
    near, sums, keep = wait((near, sums, keep))
    own_x[1], own_x[3], own_g[1], own_g[3] = near
    ends = [across(own_x[1], own_x[3], core, "z"), across(own_g[1], own_g[3], core, "x")]
    swap(1)
    swap(3)
    sums = add((1, 3), sums)
    ends, sums = wait((ends, sums))
    own_x[2], own_g[2] = ends
    swap(2)
    ht, dgt, dut, dg_own, dg_far = add((2,), sums, keep)
    dg_far = shift(dg_far, "core")
    terms = input_grads(tab, dg_own, dg_far, (gate_weight, up_weight, far_gate, far_up))
    first, second, grads, down = exchange_in_two(
        (terms[:4], "x"),
        (terms[4:], "z"),
        (
            lambda: weight_grads(token_grad_kernel, tab, (dgt, dut), own_x, far_x),
            lambda: weight_grads(down_grad_kernel, tab, (ht,), own_g, far_g),
        ),
    )
    first = exchange(sum_apart(first), "z")
    second = exchange(sum_apart(second), "x")
    parts = exchange(join_apart(first, second), "y")
    total = (parts[0].astype(F32) + parts[1].astype(F32)) + (parts[2].astype(F32) + parts[3].astype(F32))
    return (total.astype(BF16), *grads, *down)


def solution(mesh):
    return jax.shard_map(
        body,
        mesh=mesh,
        in_specs=(
            P("cuts", "shard"),
            P("cuts", "shard"),
            P("cuts"),
            P(("cuts", "shard"), None),
            P(("cuts", "shard"), None),
            P(("cuts", "shard"), None),
        ),
        out_specs=(
            P("cuts", "shard"),
            P(("cuts", "shard"), None),
            P(("cuts", "shard"), None),
            P(("cuts", "shard"), None),
        ),
        check_vma=False,
    )
```

```python
import functools

import jax
import jax.numpy as jnp
from jax import lax
from jax.experimental import pallas as pl
from jax.experimental.pallas import tpu as pltpu
from jax.sharding import PartitionSpec as P

F32 = jnp.float32
BF16 = jnp.bfloat16
NT = (((1,), (1,)), ((), ()))
NN = (((1,), (0,)), ((), ()))
SIDE = 4
wait = lax.optimization_barrier
BLOCK = 512
MIB = 2**20


def dot(a, b, dims):
    return lax.dot_general(a, b, dims, preferred_element_type=F32)


def moves(axis, step):
    if axis == "x":
        return "shard", [(z * 4 + x, z * 4 + (x + step) % 4) for z in range(4) for x in range(4)]
    if axis == "z":
        return "shard", [(z * 4 + x, (z + step) % 4 * 4 + x) for z in range(4) for x in range(4)]
    if axis == "y":
        return "cuts", [(y * 2 + c, (y + step) % 4 * 2 + c) for y in range(4) for c in range(2)]
    return "cuts", [(y * 2 + c, y * 2 + 1 - c) for y in range(4) for c in range(2)]


def hop(value, axis, way):
    pairs = []
    for y in range(4):
        for c in range(2):
            for z in range(4):
                for x in range(4):
                    step = way * (2 * c - 1)
                    to_z, to_x = (z, (x + step) % 4) if axis == "x" else ((z + step) % 4, x)
                    pairs.append(((y * 2 + c) * 16 + z * 4 + x, (y * 2 + c) * 16 + to_z * 4 + to_x))
    return lax.ppermute(value, ("cuts", "shard"), pairs)


def shift(value, axis, step=1):
    name, pairs = moves(axis, step)
    return lax.ppermute(value, name, pairs)


VMEM = pl.BlockSpec(memory_space=pltpu.VMEM)
ANY = pl.BlockSpec(memory_space=pl.ANY)
SMEM = pl.BlockSpec(memory_space=pltpu.SMEM)


def lanes(tab, at):
    return pl.ds(pl.multiple_of(tab[at] * BLOCK, BLOCK), BLOCK)


def wide(tab, at):
    return pl.ds(pl.multiple_of(tab[at] * 4 * BLOCK, 4 * BLOCK), 4 * BLOCK)


def sigmoid(v):
    return 1.0 / (1.0 + jnp.exp(-v))


def copies_of(e, tab, wg, wu, wd, bg, bu, bd, sems):
    cols = wide(tab, 32 + e)
    return [
        [pltpu.make_async_copy(wg.at[:, cols], bg, sems.at[0])],
        [pltpu.make_async_copy(wu.at[:, cols], bu, sems.at[1])],
        [pltpu.make_async_copy(wd.at[:, lanes(tab, 16 + 4 * e + d)], bd.at[d], sems.at[2 + d]) for d in range(SIDE)],
    ]


def product(total, w, data):
    for d in range(SIDE):
        term = dot(w(d), data[d], NT)
        total = term if total is None else total + term
    return total


def forward_kernel(es, first, tab, wg, wu, wd, *refs):
    refs, (bg, bu, bd, sems) = refs[:-4], refs[-4:]
    pieces, refs = refs[:4 * len(es)], refs[4 * len(es):]
    before, outs = refs[:-2], refs[-2:]
    copies = [copies_of(e, tab, wg, wu, wd, bg.at[n], bu.at[n], bd.at[n], sems.at[n]) for n, e in enumerate(es)]
    for group in copies:
        for copy in sum(group, []):
            copy.start()
    for n in range(len(es)):
        for m in range(3):
            for copy in copies[n][m]:
                copy.wait()
            w = (lambda d: bd[n, d]) if m == 2 else (lambda d: (bg, bu)[m][n, :, lanes(tab, 36 + d)])
            for side in range(2):
                total = outs[side][m] if n else None if first else before[side][m]
                outs[side][m] = product(total, w, pieces[4 * n + 2 * (m // 2) + side])


def forward(es, tab, weights, pieces, before):
    count = len(es)
    operands = [tab, *weights, *pieces, *before]
    return pl.pallas_call(
        functools.partial(forward_kernel, es, not before),
        in_specs=[SMEM] + [ANY] * 3 + [VMEM] * (len(operands) - 4),
        out_specs=[VMEM] * 2,
        out_shape=[jax.ShapeDtypeStruct((3, 224, 256), F32)] * 2,
        scratch_shapes=[
            pltpu.VMEM((count, 224, 4 * BLOCK), BF16),
            pltpu.VMEM((count, 224, 4 * BLOCK), BF16),
            pltpu.VMEM((count, 4, 224, BLOCK), BF16),
            pltpu.SemaphoreType.DMA((count, 6)),
        ],
        compiler_params=pltpu.CompilerParams(vmem_limit_bytes=(6 + 7 * count) * MIB),
        cost_estimate=pl.CostEstimate(flops=count * 6 * 512 * 224 * 2048, bytes_accessed=count * 8 * MIB, transcendentals=0),
    )(*operands)


def finish_kernel(tab, wg, wu, wd, far_wg, far_wu, far_wd, x, g, own_sums, far_sums, keep_ref, *refs):
    (own_t, far_t, own_rows, far_rows), (bg, bu, bd, sems) = refs[:4], refs[4:]
    copies = copies_of(2, tab, wg, wu, wd, bg.at[0], bu.at[0], bd, sems.at[0])
    cols = wide(tab, 34)
    far_copies = [
        [pltpu.make_async_copy(far_wg.at[:, cols], bg.at[1], sems.at[1, 0])],
        [pltpu.make_async_copy(far_wu.at[:, cols], bu.at[1], sems.at[1, 1])],
        [],
    ]
    for group in (copies, far_copies):
        for copy in sum(group, []):
            copy.start()
    for side, (group, before, out_t, out_rows) in enumerate(
        ((copies, own_sums, own_t, own_rows), (far_copies, far_sums, far_t, far_rows))
    ):
        sums = []
        for m in range(3):
            for copy in group[m]:
                copy.wait()
            down = far_wd if side else bd
            w = (lambda d: down[d]) if m == 2 else (lambda d: (bg, bu)[m][side, :, lanes(tab, 36 + d)])
            sums.append(product(before[m], w, g if m == 2 else x))
        keep = keep_ref[side:side + 1]
        gv, uv, dhv = sums[0], sums[1], sums[2] * keep
        sig = sigmoid(gv)
        silu = gv * sig
        out_t[2] = (silu * uv * keep).astype(BF16)
        dg = dhv * uv * sig * (1.0 + gv * (1.0 - sig))
        du = dhv * silu
        for k, value in enumerate((dg, du)):
            out_t[k] = value.astype(BF16)
            turned = value.T.astype(BF16)
            for b in range(SIDE):
                for half in range(2):
                    low = b * 64 + half * 32
                    out_rows[k, half, b * 32:b * 32 + 32] = turned[low:low + 32]


def finish(tab, weights, far_weights, x, g, own_sums, far_sums, keep):
    return pl.pallas_call(
        finish_kernel,
        in_specs=[SMEM] + [ANY] * 5 + [VMEM] * 6,
        out_specs=[VMEM] * 4,
        out_shape=[jax.ShapeDtypeStruct((3, 224, 256), BF16)] * 2 + [jax.ShapeDtypeStruct((2, 2, 128, 224), BF16)] * 2,
        scratch_shapes=[
            pltpu.VMEM((2, 224, 4 * BLOCK), BF16),
            pltpu.VMEM((2, 224, 4 * BLOCK), BF16),
            pltpu.VMEM((4, 224, BLOCK), BF16),
            pltpu.SemaphoreType.DMA((2, 6)),
        ],
        compiler_params=pltpu.CompilerParams(vmem_limit_bytes=16 * MIB),
        cost_estimate=pl.CostEstimate(flops=6 * 512 * 224 * 2048, bytes_accessed=8 * MIB, transcendentals=2**17),
    )(tab, *weights, *far_weights, x, g, own_sums, far_sums, keep)


def cut_down(tab, wd):
    return pl.pallas_call(
        lambda tab, w, out: out.__setitem__(0, w[...]),
        grid_spec=pltpu.PrefetchScalarGridSpec(
            num_scalar_prefetch=1,
            grid=(SIDE,),
            in_specs=[pl.BlockSpec((224, BLOCK), lambda d, tab: (0, tab[24 + d]))],
            out_specs=pl.BlockSpec((1, 224, BLOCK), lambda d, tab: (d, 0, 0)),
        ),
        out_shape=jax.ShapeDtypeStruct((4, 224, BLOCK), BF16),
        compiler_params=pltpu.CompilerParams(vmem_limit_bytes=4 * MIB),
        cost_estimate=pl.CostEstimate(flops=0, bytes_accessed=2 * MIB, transcendentals=0),
    )(tab, wd)


def token_grad_kernel(tab, own_t, far_t, *refs):
    pieces, outs = refs[:8], refs[8:]
    for e in range(SIDE):
        @pl.when(pl.program_id(0) == e)
        def _(e=e):
            for d in range(SIDE):
                x0, x1 = pieces[2 * e][d], pieces[2 * e + 1][d]
                for k, out in enumerate(outs):
                    out[:, lanes(tab, 36 + d)] = (dot(own_t[k], x0, NN) + dot(far_t[k], x1, NN)).astype(BF16)


def down_grad_kernel(tab, own_t, far_t, *refs):
    pieces, out = refs[:8], refs[8]
    d = pl.program_id(0)
    for e in range(SIDE):
        g0, g1 = pieces[2 * e][d], pieces[2 * e + 1][d]
        out[:, lanes(tab, 44 + e)] = (dot(own_t[2], g0, NN) + dot(far_t[2], g1, NN)).astype(BF16)


def weight_grads(kernel, at, count, tab, rows, own, far):
    pieces = [p for e in range(SIDE) for p in (own[e], far[e])]
    return pl.pallas_call(
        kernel,
        grid_spec=pltpu.PrefetchScalarGridSpec(
            num_scalar_prefetch=1,
            grid=(SIDE,),
            in_specs=[VMEM] * (2 + len(pieces)),
            out_specs=[pl.BlockSpec((224, 4 * BLOCK), lambda k, tab: (0, tab[at + k]))] * count,
        ),
        out_shape=[jax.ShapeDtypeStruct((224, 8192), BF16)] * count,
        compiler_params=pltpu.CompilerParams(vmem_limit_bytes=14 * MIB),
        cost_estimate=pl.CostEstimate(flops=count * 2 * 512 * 224 * 8192, bytes_accessed=count * 6 * MIB, transcendentals=0),
    )(tab, *rows, *pieces)


def input_grad_kernel(tab, own_ref, far_ref, *refs):
    weights, outs, (held, sems) = refs[:4], refs[4:12], refs[12:]
    rows = [ref[k].reshape(256, 224) for ref in (own_ref, far_ref) for k in range(2)]

    def fetch(dz):
        return [
            pltpu.make_async_copy(w.at[:, wide(tab, 32 + dz)], held.at[dz % 2, n], sems.at[dz % 2, n])
            for n, w in enumerate(weights)
        ]

    copies = fetch(0)
    for copy in copies:
        copy.start()
    for dz in range(SIDE):
        current = copies
        if dz < SIDE - 1:
            copies = fetch(dz + 1)
            for copy in copies:
                copy.start()
        for copy in current:
            copy.wait()
        for dx in range(SIDE):
            cols = lanes(tab, 44 + dx)
            w = [held[dz % 2, n, :, cols] for n in range(4)]
            total = (dot(rows[0], w[0], NN) + dot(rows[1], w[1], NN)) + (dot(rows[2], w[2], NN) + dot(rows[3], w[3], NN))
            done = total.astype(BF16)
            outs[dx][dz] = done[:128]
            outs[4 + dz][dx] = done[128:]


def input_grads(tab, own, far, weights):
    return pl.pallas_call(
        input_grad_kernel,
        in_specs=[SMEM] + [VMEM] * 2 + [ANY] * 4,
        out_specs=[VMEM] * 8,
        out_shape=[jax.ShapeDtypeStruct((4, 128, BLOCK), BF16)] * 8,
        scratch_shapes=[pltpu.VMEM((2, 4, 224, 4 * BLOCK), BF16), pltpu.SemaphoreType.DMA((2, 4))],
        compiler_params=pltpu.CompilerParams(vmem_limit_bytes=16 * MIB),
        cost_estimate=pl.CostEstimate(flops=8 * 256 * 224 * 8192, bytes_accessed=18 * MIB, transcendentals=0),
    )(tab, own, far, *weights)


def add_kernel(a, b, out):
    out[...] = (a[...].astype(F32) + b[...].astype(F32)).astype(BF16)


def add_two(a, b):
    return pl.pallas_call(
        add_kernel,
        out_shape=jax.ShapeDtypeStruct(a.shape, BF16),
        compiler_params=pltpu.CompilerParams(vmem_limit_bytes=4 * MIB),
        cost_estimate=pl.CostEstimate(flops=4 * 128 * 512, bytes_accessed=3 * 2**19, transcendentals=0),
    )(a, b)


def sum_kernel(a, b, c, *outs):
    for k in range(SIDE):
        outs[k][...] = (a[k].astype(F32) + (b[k].astype(F32) + c[k].astype(F32))).astype(BF16)


def sum_apart(parts):
    return pl.pallas_call(
        sum_kernel,
        out_shape=[jax.ShapeDtypeStruct((128, BLOCK), BF16)] * 4,
        compiler_params=pltpu.CompilerParams(vmem_limit_bytes=4 * MIB),
        cost_estimate=pl.CostEstimate(flops=3 * 4 * 128 * 512, bytes_accessed=5 * 2**19, transcendentals=0),
    )(*parts)


def join_kernel(*refs):
    ins, outs = refs[:8], refs[8:]
    for h in range(2):
        total = (ins[4 * h][...].astype(F32) + ins[4 * h + 1][...].astype(F32)) + (
            ins[4 * h + 2][...].astype(F32) + ins[4 * h + 3][...].astype(F32)
        )
        for k in range(SIDE):
            outs[k][h * 32:(h + 1) * 32] = total[k * 32:(k + 1) * 32].astype(BF16)


def join_apart(first, second):
    return pl.pallas_call(
        join_kernel,
        out_shape=[jax.ShapeDtypeStruct((64, BLOCK), BF16)] * 4,
        compiler_params=pltpu.CompilerParams(vmem_limit_bytes=4 * MIB),
        cost_estimate=pl.CostEstimate(flops=2**19, bytes_accessed=5 * 2**18, transcendentals=0),
    )(*first, *second)


def exchange(pieces, axis):
    return [pieces[0]] + [shift(pieces[d], axis, d) for d in (1, 3, 2)]


def exchange_hops(pieces, axis):
    return [pieces[0], hop(pieces[1], axis, -1), hop(pieces[3], axis, 1), shift(pieces[2], axis, 2)]


def sum_in_two(first, second, fill):
    (p, p_axis), (q, q_axis) = first, second
    sent = [hop(p[2], p_axis, -1), hop(q[2], q_axis, -1), hop(p[3], p_axis, 1), hop(q[3], q_axis, 1)]
    sent, done0 = wait((sent, fill[0]()))
    ends = [hop(add_two(p[1], sent[0]), p_axis, -1), hop(add_two(q[1], sent[1]), q_axis, -1)]
    ends, done1 = wait((ends, fill[1]()))
    return (p[0], sent[2], ends[0]), (q[0], sent[3], ends[1]), done0, done1


def around(value, axis):
    return [value] + [shift(value, axis, -e % SIDE) for e in (1, 2, 3)]


def body(tokens, grad_out, counts, gate_weight, up_weight, down_weight):
    c = lax.axis_index("cuts")
    s = lax.axis_index("shard")
    core, z, x = c % 2, s // 4, s % 4
    step = jnp.arange(SIDE, dtype=jnp.int32)
    zs, xs = (z + step) % 4, (x + step) % 4
    way = step * (1 - 2 * core)
    hop_zs, hop_xs = (z + way) % 4, (x + way) % 4
    tokens_at = hop_zs[:, None] * 4 + xs[None, :]
    grads_at = zs[None, :] * 4 + hop_xs[:, None]
    tab = jnp.concatenate([tokens_at.reshape(16), grads_at.reshape(16), hop_zs, xs, zs, hop_xs]).astype(jnp.int32)
    weights = (gate_weight, up_weight, down_weight)

    row = jnp.pad(counts.astype(BF16)[None, :], ((0, 15), (0, BLOCK - 64)))
    blocks = around(jnp.concatenate([tokens, grad_out, row], 0), "y")
    blocks, far_gate, far_up = wait((blocks, shift(gate_weight, "core"), shift(up_weight, "core")))

    x0 = jnp.concatenate([b[:64] for b in blocks], 0)
    g0 = jnp.concatenate([b[64:128] for b in blocks], 0)
    x0, g0 = wait((around(x0, "x"), around(g0, "z")))
    x0, g0 = jnp.stack(x0), jnp.stack(g0)

    own_x, own_g, far_x, far_g = {0: x0}, {0: g0}, {}, {}

    def swap(e):
        far_x[-e % SIDE], far_g[-e % SIDE] = shift(own_x[e], "core"), shift(own_g[e], "core")

    def add(es, before):
        pieces = [p[e] for e in es for p in (own_x, far_x, own_g, far_g)]
        return forward(es, tab, weights, pieces, before)

    near = [hop(x0, "z", 1), hop(x0, "z", -1), hop(g0, "x", 1), hop(g0, "x", -1)]
    swap(0)
    sums = add((0,), ())
    counts = jnp.concatenate([b[128:129, :64] for b in blocks], 1).astype(F32)
    levels = jnp.stack([c, c + 1 - 2 * core]).astype(F32)
    keep = (counts > levels[:, None]).astype(F32)
    far_down = cut_down(tab, down_weight)
    near, sums, keep, far_down = wait((near, sums, keep, far_down))
    own_x[1], own_x[3], own_g[1], own_g[3] = near
    ends = [hop(own_x[1], "z", 1), hop(own_g[1], "x", 1)]
    swap(1)
    swap(3)
    own_sums, far_sums = add((1, 3), sums)
    far_sums, far_down = shift(far_sums, "core"), shift(far_down, "core")
    ends, own_sums, far_sums, far_down = wait((ends, own_sums, far_sums, far_down))
    own_x[2], own_g[2] = ends
    swap(2)
    far_weights = (far_gate, far_up, far_down)
    own_t, far_t, own_rows, far_rows = finish(tab, weights, far_weights, own_x[2], own_g[2], own_sums, far_sums, keep)
    far_t = shift(far_t, "core")
    terms = input_grads(tab, own_rows, far_rows, (gate_weight, up_weight, far_gate, far_up))
    first, second, grads, down = sum_in_two(
        (terms[:4], "x"),
        (terms[4:], "z"),
        (
            lambda: weight_grads(token_grad_kernel, 32, 2, tab, (own_t, far_t), own_x, far_x),
            lambda: weight_grads(down_grad_kernel, 40, 1, tab, (own_t, far_t), own_g, far_g),
        ),
    )
    first = exchange_hops(sum_apart(first), "z")
    second = exchange_hops(sum_apart(second), "x")
    parts = exchange(join_apart(first, second), "y")
    total = (parts[0].astype(F32) + parts[1].astype(F32)) + (parts[2].astype(F32) + parts[3].astype(F32))
    return (total.astype(BF16), *grads, *down)


def solution(mesh):
    return jax.shard_map(
        body,
        mesh=mesh,
        in_specs=(
            P("cuts", "shard"),
            P("cuts", "shard"),
            P("cuts"),
            P(("cuts", "shard"), None),
            P(("cuts", "shard"), None),
            P(("cuts", "shard"), None),
        ),
        out_specs=(
            P("cuts", "shard"),
            P(("cuts", "shard"), None),
            P(("cuts", "shard"), None),
            P(("cuts", "shard"), None),
        ),
        check_vma=False,
    )
```

```python
import functools

import jax
import jax.numpy as jnp
from jax import lax
from jax.experimental import pallas as pl
from jax.experimental.pallas import tpu as pltpu
from jax.sharding import PartitionSpec as P

F32 = jnp.float32
BF16 = jnp.bfloat16
NT = (((1,), (1,)), ((), ()))
NN = (((1,), (0,)), ((), ()))
SIDE = 4
wait = lax.optimization_barrier
BLOCK = 512
MIB = 2**20


def dot(a, b, dims):
    return lax.dot_general(a, b, dims, preferred_element_type=F32)


def moves(axis, step):
    if axis == "x":
        return "shard", [(z * 4 + x, z * 4 + (x + step) % 4) for z in range(4) for x in range(4)]
    if axis == "z":
        return "shard", [(z * 4 + x, (z + step) % 4 * 4 + x) for z in range(4) for x in range(4)]
    if axis == "y":
        return "cuts", [(y * 2 + c, (y + step) % 4 * 2 + c) for y in range(4) for c in range(2)]
    return "cuts", [(y * 2 + c, y * 2 + 1 - c) for y in range(4) for c in range(2)]


def hop(value, axis, way):
    pairs = []
    for y in range(4):
        for c in range(2):
            for z in range(4):
                for x in range(4):
                    step = way * (2 * c - 1)
                    to_z, to_x = (z, (x + step) % 4) if axis == "x" else ((z + step) % 4, x)
                    pairs.append(((y * 2 + c) * 16 + z * 4 + x, (y * 2 + c) * 16 + to_z * 4 + to_x))
    return lax.ppermute(value, ("cuts", "shard"), pairs)


def shift(value, axis, step=1):
    name, pairs = moves(axis, step)
    return lax.ppermute(value, name, pairs)


VMEM = pl.BlockSpec(memory_space=pltpu.VMEM)
ANY = pl.BlockSpec(memory_space=pl.ANY)
SMEM = pl.BlockSpec(memory_space=pltpu.SMEM)


def lanes(tab, at):
    return pl.ds(pl.multiple_of(tab[at] * BLOCK, BLOCK), BLOCK)


def wide(tab, at):
    return pl.ds(pl.multiple_of(tab[at] * 4 * BLOCK, 4 * BLOCK), 4 * BLOCK)


def sigmoid(v):
    return 1.0 / (1.0 + jnp.exp(-v))


def copies_of(e, tab, wg, wu, wd, bg, bu, bd, sems):
    cols = wide(tab, 32 + e)
    return [
        [pltpu.make_async_copy(wg.at[:, cols], bg, sems.at[0])],
        [pltpu.make_async_copy(wu.at[:, cols], bu, sems.at[1])],
        [pltpu.make_async_copy(wd.at[:, lanes(tab, 16 + 4 * e + d)], bd.at[d], sems.at[2 + d]) for d in range(SIDE)],
    ]


def product(total, w, data):
    for d in range(SIDE):
        term = dot(w(d), data[d], NT)
        total = term if total is None else total + term
    return total


def forward_kernel(es, first, tab, wg, wu, wd, *refs):
    refs, (bg, bu, bd, sems) = refs[:-4], refs[-4:]
    pieces, refs = refs[:4 * len(es)], refs[4 * len(es):]
    before, outs = refs[:-2], refs[-2:]
    copies = [copies_of(e, tab, wg, wu, wd, bg.at[n], bu.at[n], bd.at[n], sems.at[n]) for n, e in enumerate(es)]
    for group in copies:
        for copy in sum(group, []):
            copy.start()
    for n in range(len(es)):
        for m in range(3):
            for copy in copies[n][m]:
                copy.wait()
            w = (lambda d: bd[n, d]) if m == 2 else (lambda d: (bg, bu)[m][n, :, lanes(tab, 36 + d)])
            for side in range(2):
                total = outs[side][m] if n else None if first else before[side][m]
                outs[side][m] = product(total, w, pieces[4 * n + 2 * (m // 2) + side])


def forward(es, tab, weights, pieces, before):
    count = len(es)
    operands = [tab, *weights, *pieces, *before]
    return pl.pallas_call(
        functools.partial(forward_kernel, es, not before),
        in_specs=[SMEM] + [ANY] * 3 + [VMEM] * (len(operands) - 4),
        out_specs=[VMEM] * 2,
        out_shape=[jax.ShapeDtypeStruct((3, 224, 256), F32)] * 2,
        scratch_shapes=[
            pltpu.VMEM((count, 224, 4 * BLOCK), BF16),
            pltpu.VMEM((count, 224, 4 * BLOCK), BF16),
            pltpu.VMEM((count, 4, 224, BLOCK), BF16),
            pltpu.SemaphoreType.DMA((count, 6)),
        ],
        compiler_params=pltpu.CompilerParams(vmem_limit_bytes=(6 + 7 * count) * MIB),
        cost_estimate=pl.CostEstimate(flops=count * 6 * 512 * 224 * 2048, bytes_accessed=count * 8 * MIB, transcendentals=0),
    )(*operands)


def finish_kernel(tab, wg, wu, wd, far_wg, far_wu, far_wd, x, g, own_sums, far_sums, keep_ref, *refs):
    (own_t, far_t, own_rows, far_rows), (bg, bu, bd, sems) = refs[:4], refs[4:]
    copies = copies_of(2, tab, wg, wu, wd, bg.at[0], bu.at[0], bd, sems.at[0])
    cols = wide(tab, 34)
    far_copies = [
        [pltpu.make_async_copy(far_wg.at[:, cols], bg.at[1], sems.at[1, 0])],
        [pltpu.make_async_copy(far_wu.at[:, cols], bu.at[1], sems.at[1, 1])],
        [],
    ]
    for group in (copies, far_copies):
        for copy in sum(group, []):
            copy.start()
    for side, (group, before, out_t, out_rows) in enumerate(
        ((copies, own_sums, own_t, own_rows), (far_copies, far_sums, far_t, far_rows))
    ):
        sums = []
        for m in range(3):
            for copy in group[m]:
                copy.wait()
            down = far_wd if side else bd
            w = (lambda d: down[d]) if m == 2 else (lambda d: (bg, bu)[m][side, :, lanes(tab, 36 + d)])
            sums.append(product(before[m], w, g if m == 2 else x))
        keep = keep_ref[side:side + 1]
        gv, uv, dhv = sums[0], sums[1], sums[2] * keep
        sig = sigmoid(gv)
        silu = gv * sig
        out_t[2] = (silu * uv * keep).astype(BF16)
        dg = dhv * uv * sig * (1.0 + gv * (1.0 - sig))
        du = dhv * silu
        for k, value in enumerate((dg, du)):
            out_t[k] = value.astype(BF16)
            turned = value.T.astype(BF16)
            for b in range(SIDE):
                for half in range(2):
                    low = b * 64 + half * 32
                    out_rows[k, half, b * 32:b * 32 + 32] = turned[low:low + 32]


def finish(tab, weights, far_weights, x, g, own_sums, far_sums, keep):
    return pl.pallas_call(
        finish_kernel,
        in_specs=[SMEM] + [ANY] * 5 + [VMEM] * 6,
        out_specs=[VMEM] * 4,
        out_shape=[jax.ShapeDtypeStruct((3, 224, 256), BF16)] * 2 + [jax.ShapeDtypeStruct((2, 2, 128, 224), BF16)] * 2,
        scratch_shapes=[
            pltpu.VMEM((2, 224, 4 * BLOCK), BF16),
            pltpu.VMEM((2, 224, 4 * BLOCK), BF16),
            pltpu.VMEM((4, 224, BLOCK), BF16),
            pltpu.SemaphoreType.DMA((2, 6)),
        ],
        compiler_params=pltpu.CompilerParams(vmem_limit_bytes=16 * MIB),
        cost_estimate=pl.CostEstimate(flops=6 * 512 * 224 * 2048, bytes_accessed=8 * MIB, transcendentals=2**17),
    )(tab, *weights, *far_weights, x, g, own_sums, far_sums, keep)


def cut_down(tab, wd):
    return pl.pallas_call(
        lambda tab, w, out: out.__setitem__(0, w[...]),
        grid_spec=pltpu.PrefetchScalarGridSpec(
            num_scalar_prefetch=1,
            grid=(SIDE,),
            in_specs=[pl.BlockSpec((224, BLOCK), lambda d, tab: (0, tab[24 + d]))],
            out_specs=pl.BlockSpec((1, 224, BLOCK), lambda d, tab: (d, 0, 0)),
        ),
        out_shape=jax.ShapeDtypeStruct((4, 224, BLOCK), BF16),
        compiler_params=pltpu.CompilerParams(vmem_limit_bytes=4 * MIB),
        cost_estimate=pl.CostEstimate(flops=0, bytes_accessed=2 * MIB, transcendentals=0),
    )(tab, wd)


def token_grad_kernel(tab, own_t, far_t, *refs):
    pieces, outs = refs[:8], refs[8:]
    for e in range(SIDE):
        @pl.when(pl.program_id(0) == e)
        def _(e=e):
            for d in range(SIDE):
                x0, x1 = pieces[2 * e][d], pieces[2 * e + 1][d]
                for k, out in enumerate(outs):
                    out[:, lanes(tab, 36 + d)] = (dot(own_t[k], x0, NN) + dot(far_t[k], x1, NN)).astype(BF16)


def down_grad_kernel(tab, own_t, far_t, *refs):
    pieces, out = refs[:8], refs[8]
    d = pl.program_id(0)
    for e in range(SIDE):
        g0, g1 = pieces[2 * e][d], pieces[2 * e + 1][d]
        out[:, lanes(tab, 44 + e)] = (dot(own_t[2], g0, NN) + dot(far_t[2], g1, NN)).astype(BF16)


def weight_grads(kernel, at, count, tab, rows, own, far):
    pieces = [p for e in range(SIDE) for p in (own[e], far[e])]
    return pl.pallas_call(
        kernel,
        grid_spec=pltpu.PrefetchScalarGridSpec(
            num_scalar_prefetch=1,
            grid=(SIDE,),
            in_specs=[VMEM] * (2 + len(pieces)),
            out_specs=[pl.BlockSpec((224, 4 * BLOCK), lambda k, tab: (0, tab[at + k]))] * count,
        ),
        out_shape=[jax.ShapeDtypeStruct((224, 8192), BF16)] * count,
        compiler_params=pltpu.CompilerParams(vmem_limit_bytes=14 * MIB),
        cost_estimate=pl.CostEstimate(flops=count * 2 * 512 * 224 * 8192, bytes_accessed=count * 6 * MIB, transcendentals=0),
    )(tab, *rows, *pieces)


def input_grad_kernel(tab, own_ref, far_ref, *refs):
    weights, outs, (held, sems) = refs[:4], refs[4:12], refs[12:]
    rows = [ref[k].reshape(256, 224) for ref in (own_ref, far_ref) for k in range(2)]

    def fetch(dz):
        return [
            pltpu.make_async_copy(w.at[:, wide(tab, 32 + dz)], held.at[dz % 2, n], sems.at[dz % 2, n])
            for n, w in enumerate(weights)
        ]

    copies = fetch(0)
    for copy in copies:
        copy.start()
    for dz in range(SIDE):
        current = copies
        if dz < SIDE - 1:
            copies = fetch(dz + 1)
            for copy in copies:
                copy.start()
        for copy in current:
            copy.wait()
        for dx in range(SIDE):
            cols = lanes(tab, 44 + dx)
            w = [held[dz % 2, n, :, cols] for n in range(4)]
            total = (dot(rows[0], w[0], NN) + dot(rows[1], w[1], NN)) + (dot(rows[2], w[2], NN) + dot(rows[3], w[3], NN))
            done = total.astype(BF16)
            outs[dx][dz] = done[:128]
            outs[4 + dz][dx] = done[128:]


def input_grads(tab, own, far, weights):
    return pl.pallas_call(
        input_grad_kernel,
        in_specs=[SMEM] + [VMEM] * 2 + [ANY] * 4,
        out_specs=[VMEM] * 8,
        out_shape=[jax.ShapeDtypeStruct((4, 128, BLOCK), BF16)] * 8,
        scratch_shapes=[pltpu.VMEM((2, 4, 224, 4 * BLOCK), BF16), pltpu.SemaphoreType.DMA((2, 4))],
        compiler_params=pltpu.CompilerParams(vmem_limit_bytes=16 * MIB),
        cost_estimate=pl.CostEstimate(flops=8 * 256 * 224 * 8192, bytes_accessed=18 * MIB, transcendentals=0),
    )(tab, own, far, *weights)


def add_kernel(a, b, out):
    out[...] = (a[...].astype(F32) + b[...].astype(F32)).astype(BF16)


def add_two(a, b):
    return pl.pallas_call(
        add_kernel,
        out_shape=jax.ShapeDtypeStruct(a.shape, BF16),
        compiler_params=pltpu.CompilerParams(vmem_limit_bytes=4 * MIB),
        cost_estimate=pl.CostEstimate(flops=4 * 128 * 512, bytes_accessed=3 * 2**19, transcendentals=0),
    )(a, b)


def sum_kernel(a, b, c, *outs):
    for k in range(SIDE):
        outs[k][...] = (a[k].astype(F32) + (b[k].astype(F32) + c[k].astype(F32))).astype(BF16)


def sum_apart(parts):
    return pl.pallas_call(
        sum_kernel,
        out_shape=[jax.ShapeDtypeStruct((128, BLOCK), BF16)] * 4,
        compiler_params=pltpu.CompilerParams(vmem_limit_bytes=4 * MIB),
        cost_estimate=pl.CostEstimate(flops=3 * 4 * 128 * 512, bytes_accessed=5 * 2**19, transcendentals=0),
    )(*parts)


def join_kernel(*refs):
    ins, outs = refs[:8], refs[8:]
    for h in range(2):
        total = (ins[4 * h][...].astype(F32) + ins[4 * h + 1][...].astype(F32)) + (
            ins[4 * h + 2][...].astype(F32) + ins[4 * h + 3][...].astype(F32)
        )
        for k in range(SIDE):
            outs[k][h * 32:(h + 1) * 32] = total[k * 32:(k + 1) * 32].astype(BF16)


def join_apart(first, second):
    return pl.pallas_call(
        join_kernel,
        out_shape=[jax.ShapeDtypeStruct((64, BLOCK), BF16)] * 4,
        compiler_params=pltpu.CompilerParams(vmem_limit_bytes=4 * MIB),
        cost_estimate=pl.CostEstimate(flops=2**19, bytes_accessed=5 * 2**18, transcendentals=0),
    )(*first, *second)


def exchange(pieces, axis):
    far = shift(pieces[2], axis, 2)
    return [pieces[0], far, shift(pieces[1], axis, 1), shift(pieces[3], axis, 3)]


def exchange_hops(pieces, axis):
    far = shift(pieces[2], axis, 2)
    return [pieces[0], far, hop(pieces[1], axis, -1), hop(pieces[3], axis, 1)]


def sum_in_two(first, second, fill):
    (p, p_axis), (q, q_axis) = first, second
    sent = [hop(p[2], p_axis, -1), hop(q[2], q_axis, -1), hop(p[3], p_axis, 1), hop(q[3], q_axis, 1)]
    sent, done0 = wait((sent, fill[0]()))
    ends = [hop(add_two(p[1], sent[0]), p_axis, -1), hop(add_two(q[1], sent[1]), q_axis, -1)]
    ends, done1 = wait((ends, fill[1]()))
    return (p[0], sent[2], ends[0]), (q[0], sent[3], ends[1]), done0, done1


def around(value, axis):
    near = shift(value, axis, 3), shift(value, axis, 1)
    return [value, near[0], shift(value, axis, 2), near[1]]


def body(tokens, grad_out, counts, gate_weight, up_weight, down_weight):
    c = lax.axis_index("cuts")
    s = lax.axis_index("shard")
    core, z, x = c % 2, s // 4, s % 4
    step = jnp.arange(SIDE, dtype=jnp.int32)
    zs, xs = (z + step) % 4, (x + step) % 4
    way = step * (1 - 2 * core)
    hop_zs, hop_xs = (z + way) % 4, (x + way) % 4
    tokens_at = hop_zs[:, None] * 4 + xs[None, :]
    grads_at = zs[None, :] * 4 + hop_xs[:, None]
    tab = jnp.concatenate([tokens_at.reshape(16), grads_at.reshape(16), hop_zs, xs, zs, hop_xs]).astype(jnp.int32)
    weights = (gate_weight, up_weight, down_weight)

    row = jnp.pad(counts.astype(BF16)[None, :], ((0, 15), (0, BLOCK - 64)))
    blocks = around(jnp.concatenate([tokens, grad_out, row], 0), "y")
    blocks, far_gate = wait((blocks, shift(gate_weight, "core")))

    x0 = jnp.concatenate([b[:64] for b in blocks], 0)
    g0 = jnp.concatenate([b[64:128] for b in blocks], 0)
    g0, far_up = wait((g0, shift(up_weight, "core")))
    g0, x0 = wait((around(g0, "z"), around(x0, "x")))
    x0, g0 = jnp.stack(x0), jnp.stack(g0)

    own_x, own_g, far_x, far_g = {0: x0}, {0: g0}, {}, {}

    def swap(e):
        far_x[-e % SIDE], far_g[-e % SIDE] = shift(own_x[e], "core"), shift(own_g[e], "core")

    def add(es, before):
        pieces = [p[e] for e in es for p in (own_x, far_x, own_g, far_g)]
        return forward(es, tab, weights, pieces, before)

    near = [hop(x0, "z", 1), hop(x0, "z", -1), hop(g0, "x", 1), hop(g0, "x", -1)]
    swap(0)
    sums = add((0,), ())
    counts = jnp.concatenate([b[128:129, :64] for b in blocks], 1).astype(F32)
    levels = jnp.stack([c, c + 1 - 2 * core]).astype(F32)
    keep = (counts > levels[:, None]).astype(F32)
    far_down = cut_down(tab, down_weight)
    near, sums, keep, far_down = wait((near, sums, keep, far_down))
    own_x[1], own_x[3], own_g[1], own_g[3] = near
    swap(1)
    swap(3)
    ends = [hop(own_x[1], "z", 1), hop(own_g[1], "x", 1)]
    own_sums, far_sums = add((1, 3), sums)
    far_sums, far_down = shift(far_sums, "core"), shift(far_down, "core")
    ends, own_sums, far_sums, far_down = wait((ends, own_sums, far_sums, far_down))
    own_x[2], own_g[2] = ends
    swap(2)
    far_weights = (far_gate, far_up, far_down)
    own_t, far_t, own_rows, far_rows = finish(tab, weights, far_weights, own_x[2], own_g[2], own_sums, far_sums, keep)
    far_t = shift(far_t, "core")
    terms = input_grads(tab, own_rows, far_rows, (gate_weight, up_weight, far_gate, far_up))
    first, second, grads, down = sum_in_two(
        (terms[:4], "x"),
        (terms[4:], "z"),
        (
            lambda: weight_grads(token_grad_kernel, 32, 2, tab, (own_t, far_t), own_x, far_x),
            lambda: weight_grads(down_grad_kernel, 40, 1, tab, (own_t, far_t), own_g, far_g),
        ),
    )
    first = exchange_hops(sum_apart(first), "z")
    second = exchange_hops(sum_apart(second), "x")
    parts = exchange(join_apart(first, second), "y")
    total = (parts[0].astype(F32) + parts[1].astype(F32)) + (parts[2].astype(F32) + parts[3].astype(F32))
    return (total.astype(BF16), *grads, *down)


def solution(mesh):
    return jax.shard_map(
        body,
        mesh=mesh,
        in_specs=(
            P("cuts", "shard"),
            P("cuts", "shard"),
            P("cuts"),
            P(("cuts", "shard"), None),
            P(("cuts", "shard"), None),
            P(("cuts", "shard"), None),
        ),
        out_specs=(
            P("cuts", "shard"),
            P(("cuts", "shard"), None),
            P(("cuts", "shard"), None),
            P(("cuts", "shard"), None),
        ),
        check_vma=False,
    )
```

```python
import functools

import jax
import jax.numpy as jnp
from jax import lax
from jax.experimental import pallas as pl
from jax.experimental.pallas import tpu as pltpu
from jax.sharding import PartitionSpec as P

F32 = jnp.float32
BF16 = jnp.bfloat16
NT = (((1,), (1,)), ((), ()))
NN = (((1,), (0,)), ((), ()))
SIDE = 4
wait = lax.optimization_barrier
BLOCK = 512
MIB = 2**20


def dot(a, b, dims):
    return lax.dot_general(a, b, dims, preferred_element_type=F32)


def moves(axis, step):
    if axis == "x":
        return "shard", [(z * 4 + x, z * 4 + (x + step) % 4) for z in range(4) for x in range(4)]
    if axis == "z":
        return "shard", [(z * 4 + x, (z + step) % 4 * 4 + x) for z in range(4) for x in range(4)]
    if axis == "y":
        return "cuts", [(y * 2 + c, (y + step) % 4 * 2 + c) for y in range(4) for c in range(2)]
    return "cuts", [(y * 2 + c, y * 2 + 1 - c) for y in range(4) for c in range(2)]


def hop(value, axis, way):
    pairs = []
    for y in range(4):
        for c in range(2):
            for z in range(4):
                for x in range(4):
                    step = way * (2 * c - 1)
                    to_z, to_x = (z, (x + step) % 4) if axis == "x" else ((z + step) % 4, x)
                    pairs.append(((y * 2 + c) * 16 + z * 4 + x, (y * 2 + c) * 16 + to_z * 4 + to_x))
    return lax.ppermute(value, ("cuts", "shard"), pairs)


def shift(value, axis, step=1):
    name, pairs = moves(axis, step)
    return lax.ppermute(value, name, pairs)


VMEM = pl.BlockSpec(memory_space=pltpu.VMEM)
ANY = pl.BlockSpec(memory_space=pl.ANY)
SMEM = pl.BlockSpec(memory_space=pltpu.SMEM)


def lanes(tab, at):
    return pl.ds(pl.multiple_of(tab[at] * BLOCK, BLOCK), BLOCK)


def wide(tab, at):
    return pl.ds(pl.multiple_of(tab[at] * 4 * BLOCK, 4 * BLOCK), 4 * BLOCK)


def sigmoid(v):
    return 1.0 / (1.0 + jnp.exp(-v))


def copies_of(e, tab, wg, wu, wd, bg, bu, bd, sems):
    cols = wide(tab, 32 + e)
    return [
        [pltpu.make_async_copy(wg.at[:, cols], bg, sems.at[0])],
        [pltpu.make_async_copy(wu.at[:, cols], bu, sems.at[1])],
        [pltpu.make_async_copy(wd.at[:, lanes(tab, 16 + 4 * e + d)], bd.at[d], sems.at[2 + d]) for d in range(SIDE)],
    ]


def product(total, w, data):
    for d in range(SIDE):
        term = dot(w(d), data[d], NT)
        total = term if total is None else total + term
    return total


def forward_kernel(es, first, tab, wg, wu, wd, *refs):
    refs, (bg, bu, bd, sems) = refs[:-4], refs[-4:]
    pieces, refs = refs[:4 * len(es)], refs[4 * len(es):]
    before, outs = refs[:-2], refs[-2:]
    copies = [copies_of(e, tab, wg, wu, wd, bg.at[n], bu.at[n], bd.at[n], sems.at[n]) for n, e in enumerate(es)]
    for group in copies:
        for copy in sum(group, []):
            copy.start()
    for n in range(len(es)):
        for m in range(3):
            for copy in copies[n][m]:
                copy.wait()
            w = (lambda d: bd[n, d]) if m == 2 else (lambda d: (bg, bu)[m][n, :, lanes(tab, 36 + d)])
            for side in range(2):
                total = outs[side][m] if n else None if first else before[side][m]
                outs[side][m] = product(total, w, pieces[4 * n + 2 * (m // 2) + side])


def forward(es, tab, weights, pieces, before):
    count = len(es)
    operands = [tab, *weights, *pieces, *before]
    return pl.pallas_call(
        functools.partial(forward_kernel, es, not before),
        in_specs=[SMEM] + [ANY] * 3 + [VMEM] * (len(operands) - 4),
        out_specs=[VMEM] * 2,
        out_shape=[jax.ShapeDtypeStruct((3, 224, 256), F32)] * 2,
        scratch_shapes=[
            pltpu.VMEM((count, 224, 4 * BLOCK), BF16),
            pltpu.VMEM((count, 224, 4 * BLOCK), BF16),
            pltpu.VMEM((count, 4, 224, BLOCK), BF16),
            pltpu.SemaphoreType.DMA((count, 6)),
        ],
        compiler_params=pltpu.CompilerParams(vmem_limit_bytes=(6 + 7 * count) * MIB),
        cost_estimate=pl.CostEstimate(flops=count * 6 * 512 * 224 * 2048, bytes_accessed=count * 8 * MIB, transcendentals=0),
    )(*operands)


def finish_kernel(tab, wg, wu, wd, far_wg, far_wu, far_wd, x, g, own_sums, far_sums, keep_ref, *refs):
    (own_t, far_t, own_rows, far_rows), (bg, bu, bd, sems) = refs[:4], refs[4:]
    copies = copies_of(2, tab, wg, wu, wd, bg.at[0], bu.at[0], bd, sems.at[0])
    cols = wide(tab, 34)
    far_copies = [
        [pltpu.make_async_copy(far_wg.at[:, cols], bg.at[1], sems.at[1, 0])],
        [pltpu.make_async_copy(far_wu.at[:, cols], bu.at[1], sems.at[1, 1])],
        [],
    ]
    for group in (copies, far_copies):
        for copy in sum(group, []):
            copy.start()
    for side, (group, before, out_t, out_rows) in enumerate(
        ((copies, own_sums, own_t, own_rows), (far_copies, far_sums, far_t, far_rows))
    ):
        sums = []
        for m in range(3):
            for copy in group[m]:
                copy.wait()
            down = far_wd if side else bd
            w = (lambda d: down[d]) if m == 2 else (lambda d: (bg, bu)[m][side, :, lanes(tab, 36 + d)])
            sums.append(product(before[m], w, g if m == 2 else x))
        keep = keep_ref[side:side + 1]
        gv, uv, dhv = sums[0], sums[1], sums[2] * keep
        sig = sigmoid(gv)
        silu = gv * sig
        out_t[2] = (silu * uv * keep).astype(BF16)
        dg = dhv * uv * sig * (1.0 + gv * (1.0 - sig))
        du = dhv * silu
        for k, value in enumerate((dg, du)):
            out_t[k] = value.astype(BF16)
            turned = value.T.astype(BF16)
            for b in range(SIDE):
                for half in range(2):
                    low = b * 64 + half * 32
                    out_rows[k, half, b * 32:b * 32 + 32] = turned[low:low + 32]


def finish(tab, weights, far_weights, x, g, own_sums, far_sums, keep):
    return pl.pallas_call(
        finish_kernel,
        in_specs=[SMEM] + [ANY] * 5 + [VMEM] * 6,
        out_specs=[VMEM] * 4,
        out_shape=[jax.ShapeDtypeStruct((3, 224, 256), BF16)] * 2 + [jax.ShapeDtypeStruct((2, 2, 128, 224), BF16)] * 2,
        scratch_shapes=[
            pltpu.VMEM((2, 224, 4 * BLOCK), BF16),
            pltpu.VMEM((2, 224, 4 * BLOCK), BF16),
            pltpu.VMEM((4, 224, BLOCK), BF16),
            pltpu.SemaphoreType.DMA((2, 6)),
        ],
        compiler_params=pltpu.CompilerParams(vmem_limit_bytes=16 * MIB),
        cost_estimate=pl.CostEstimate(flops=6 * 512 * 224 * 2048, bytes_accessed=8 * MIB, transcendentals=2**17),
    )(tab, *weights, *far_weights, x, g, own_sums, far_sums, keep)


def cut_down(tab, wd):
    return pl.pallas_call(
        lambda tab, w, out: out.__setitem__(0, w[...]),
        grid_spec=pltpu.PrefetchScalarGridSpec(
            num_scalar_prefetch=1,
            grid=(SIDE,),
            in_specs=[pl.BlockSpec((224, BLOCK), lambda d, tab: (0, tab[24 + d]))],
            out_specs=pl.BlockSpec((1, 224, BLOCK), lambda d, tab: (d, 0, 0)),
        ),
        out_shape=jax.ShapeDtypeStruct((4, 224, BLOCK), BF16),
        compiler_params=pltpu.CompilerParams(vmem_limit_bytes=4 * MIB),
        cost_estimate=pl.CostEstimate(flops=0, bytes_accessed=2 * MIB, transcendentals=0),
    )(tab, wd)


def token_grad_kernel(tab, own_t, far_t, *refs):
    pieces, outs = refs[:8], refs[8:]
    for e in range(SIDE):
        @pl.when(pl.program_id(0) == e)
        def _(e=e):
            for d in range(SIDE):
                x0, x1 = pieces[2 * e][d], pieces[2 * e + 1][d]
                for k, out in enumerate(outs):
                    out[:, lanes(tab, 36 + d)] = (dot(own_t[k], x0, NN) + dot(far_t[k], x1, NN)).astype(BF16)


def down_grad_kernel(tab, own_t, far_t, *refs):
    pieces, out = refs[:8], refs[8]
    d = pl.program_id(0)
    for e in range(SIDE):
        g0, g1 = pieces[2 * e][d], pieces[2 * e + 1][d]
        out[:, lanes(tab, 44 + e)] = (dot(own_t[2], g0, NN) + dot(far_t[2], g1, NN)).astype(BF16)


def weight_grads(kernel, at, count, tab, rows, own, far):
    pieces = [p for e in range(SIDE) for p in (own[e], far[e])]
    return pl.pallas_call(
        kernel,
        grid_spec=pltpu.PrefetchScalarGridSpec(
            num_scalar_prefetch=1,
            grid=(SIDE,),
            in_specs=[VMEM] * (2 + len(pieces)),
            out_specs=[pl.BlockSpec((224, 4 * BLOCK), lambda k, tab: (0, tab[at + k]))] * count,
        ),
        out_shape=[jax.ShapeDtypeStruct((224, 8192), BF16)] * count,
        compiler_params=pltpu.CompilerParams(vmem_limit_bytes=14 * MIB),
        cost_estimate=pl.CostEstimate(flops=count * 2 * 512 * 224 * 8192, bytes_accessed=count * 6 * MIB, transcendentals=0),
    )(tab, *rows, *pieces)


def input_grad_kernel(tab, own_ref, far_ref, *refs):
    weights, outs, (held, sems) = refs[:4], refs[4:12], refs[12:]
    rows = [ref[k].reshape(256, 224) for ref in (own_ref, far_ref) for k in range(2)]

    def fetch(dz):
        return [
            pltpu.make_async_copy(w.at[:, wide(tab, 32 + dz)], held.at[dz % 2, n], sems.at[dz % 2, n])
            for n, w in enumerate(weights)
        ]

    copies = fetch(0)
    for copy in copies:
        copy.start()
    for dz in range(SIDE):
        current = copies
        if dz < SIDE - 1:
            copies = fetch(dz + 1)
            for copy in copies:
                copy.start()
        for copy in current:
            copy.wait()
        for dx in range(SIDE):
            cols = lanes(tab, 44 + dx)
            w = [held[dz % 2, n, :, cols] for n in range(4)]
            total = (dot(rows[0], w[0], NN) + dot(rows[1], w[1], NN)) + (dot(rows[2], w[2], NN) + dot(rows[3], w[3], NN))
            done = total.astype(BF16)
            outs[dx][dz] = done[:128]
            outs[4 + dz][dx] = done[128:]


def input_grads(tab, own, far, weights):
    return pl.pallas_call(
        input_grad_kernel,
        in_specs=[SMEM] + [VMEM] * 2 + [ANY] * 4,
        out_specs=[VMEM] * 8,
        out_shape=[jax.ShapeDtypeStruct((4, 128, BLOCK), BF16)] * 8,
        scratch_shapes=[pltpu.VMEM((2, 4, 224, 4 * BLOCK), BF16), pltpu.SemaphoreType.DMA((2, 4))],
        compiler_params=pltpu.CompilerParams(vmem_limit_bytes=16 * MIB),
        cost_estimate=pl.CostEstimate(flops=8 * 256 * 224 * 8192, bytes_accessed=18 * MIB, transcendentals=0),
    )(tab, own, far, *weights)


def add_kernel(a, b, out):
    out[...] = (a[...].astype(F32) + b[...].astype(F32)).astype(BF16)


def add_two(a, b):
    return pl.pallas_call(
        add_kernel,
        out_shape=jax.ShapeDtypeStruct(a.shape, BF16),
        compiler_params=pltpu.CompilerParams(vmem_limit_bytes=4 * MIB),
        cost_estimate=pl.CostEstimate(flops=4 * 128 * 512, bytes_accessed=3 * 2**19, transcendentals=0),
    )(a, b)


def sum_kernel(a, b, c, *outs):
    for k in range(SIDE):
        outs[k][...] = (a[k].astype(F32) + (b[k].astype(F32) + c[k].astype(F32))).astype(BF16)


def sum_apart(parts):
    return pl.pallas_call(
        sum_kernel,
        out_shape=[jax.ShapeDtypeStruct((128, BLOCK), BF16)] * 4,
        compiler_params=pltpu.CompilerParams(vmem_limit_bytes=4 * MIB),
        cost_estimate=pl.CostEstimate(flops=3 * 4 * 128 * 512, bytes_accessed=5 * 2**19, transcendentals=0),
    )(*parts)


def join_kernel(*refs):
    ins, outs = refs[:8], refs[8:]
    for h in range(2):
        total = (ins[4 * h][...].astype(F32) + ins[4 * h + 1][...].astype(F32)) + (
            ins[4 * h + 2][...].astype(F32) + ins[4 * h + 3][...].astype(F32)
        )
        for k in range(SIDE):
            outs[k][h * 32:(h + 1) * 32] = total[k * 32:(k + 1) * 32].astype(BF16)


def join_apart(first, second):
    return pl.pallas_call(
        join_kernel,
        out_shape=[jax.ShapeDtypeStruct((64, BLOCK), BF16)] * 4,
        compiler_params=pltpu.CompilerParams(vmem_limit_bytes=4 * MIB),
        cost_estimate=pl.CostEstimate(flops=2**19, bytes_accessed=5 * 2**18, transcendentals=0),
    )(*first, *second)


def exchange(pieces, axis):
    far = shift(pieces[2], axis, 2)
    return [pieces[0], far, shift(pieces[1], axis, 1), shift(pieces[3], axis, 3)]


def exchange_hops(pieces, axis):
    far = shift(pieces[2], axis, 2)
    return [pieces[0], far, hop(pieces[1], axis, -1), hop(pieces[3], axis, 1)]


def sum_in_two(first, second, fill):
    (p, p_axis), (q, q_axis) = first, second
    sent = [hop(p[2], p_axis, -1), hop(q[2], q_axis, -1), hop(p[3], p_axis, 1), hop(q[3], q_axis, 1)]
    sent, done0 = wait((sent, fill[0]()))
    ends = [hop(add_two(p[1], sent[0]), p_axis, -1), hop(add_two(q[1], sent[1]), q_axis, -1)]
    ends, done1 = wait((ends, fill[1]()))
    return (p[0], sent[2], ends[0]), (q[0], sent[3], ends[1]), done0, done1


def around(value, axis):
    near = shift(value, axis, 3), shift(value, axis, 1)
    return [value, near[0], shift(value, axis, 2), near[1]]


def body(tokens, grad_out, counts, gate_weight, up_weight, down_weight):
    c = lax.axis_index("cuts")
    s = lax.axis_index("shard")
    core, z, x = c % 2, s // 4, s % 4
    step = jnp.arange(SIDE, dtype=jnp.int32)
    zs, xs = (z + step) % 4, (x + step) % 4
    way = step * (1 - 2 * core)
    hop_zs, hop_xs = (z + way) % 4, (x + way) % 4
    tokens_at = hop_zs[:, None] * 4 + xs[None, :]
    grads_at = zs[None, :] * 4 + hop_xs[:, None]
    tab = jnp.concatenate([tokens_at.reshape(16), grads_at.reshape(16), hop_zs, xs, zs, hop_xs]).astype(jnp.int32)
    weights = (gate_weight, up_weight, down_weight)

    row = jnp.pad(counts.astype(BF16)[None, :], ((0, 15), (0, BLOCK - 64)))
    blocks = around(jnp.concatenate([tokens, grad_out, row], 0), "y")
    blocks, far_gate = wait((blocks, shift(gate_weight, "core")))

    x0 = jnp.concatenate([b[:64] for b in blocks], 0)
    g0 = jnp.concatenate([b[64:128] for b in blocks], 0)
    g0, far_up = wait((g0, shift(up_weight, "core")))
    g0, x0 = wait((around(g0, "z"), around(x0, "x")))
    x0, g0 = jnp.stack(x0), jnp.stack(g0)

    own_x, own_g, far_x, far_g = {0: x0}, {0: g0}, {}, {}

    def swap(e):
        far_x[-e % SIDE], far_g[-e % SIDE] = shift(own_x[e], "core"), shift(own_g[e], "core")

    def add(es, before):
        pieces = [p[e] for e in es for p in (own_x, far_x, own_g, far_g)]
        return forward(es, tab, weights, pieces, before)

    near = [hop(x0, "z", 1), hop(x0, "z", -1), hop(g0, "x", 1), hop(g0, "x", -1)]
    swap(0)
    sums = add((0,), ())
    counts = jnp.concatenate([b[128:129, :64] for b in blocks], 1).astype(F32)
    levels = jnp.stack([c, c + 1 - 2 * core]).astype(F32)
    keep = (counts > levels[:, None]).astype(F32)
    far_down = cut_down(tab, down_weight)
    near, sums, keep, far_down = wait((near, sums, keep, far_down))
    own_x[1], own_x[3], own_g[1], own_g[3] = near
    swap(1)
    own_g[3], _ = wait((own_g[3], far_x[3]))
    swap(3)
    ends = [hop(own_x[1], "z", 1), hop(own_g[1], "x", 1)]
    own_sums, far_sums = add((1, 3), sums)
    far_sums, far_down = shift(far_sums, "core"), shift(far_down, "core")
    ends, own_sums, far_sums, far_down = wait((ends, own_sums, far_sums, far_down))
    own_x[2], own_g[2] = ends
    swap(2)
    far_weights = (far_gate, far_up, far_down)
    own_t, far_t, own_rows, far_rows = finish(tab, weights, far_weights, own_x[2], own_g[2], own_sums, far_sums, keep)
    far_t = shift(far_t, "core")
    terms = input_grads(tab, own_rows, far_rows, (gate_weight, up_weight, far_gate, far_up))
    first, second, grads, down = sum_in_two(
        (terms[:4], "x"),
        (terms[4:], "z"),
        (
            lambda: weight_grads(token_grad_kernel, 32, 2, tab, (own_t, far_t), own_x, far_x),
            lambda: weight_grads(down_grad_kernel, 40, 1, tab, (own_t, far_t), own_g, far_g),
        ),
    )
    first = exchange_hops(sum_apart(first), "z")
    second = exchange_hops(sum_apart(second), "x")
    parts = exchange(join_apart(first, second), "y")
    total = (parts[0].astype(F32) + parts[1].astype(F32)) + (parts[2].astype(F32) + parts[3].astype(F32))
    return (total.astype(BF16), *grads, *down)


def solution(mesh):
    return jax.shard_map(
        body,
        mesh=mesh,
        in_specs=(
            P("cuts", "shard"),
            P("cuts", "shard"),
            P("cuts"),
            P(("cuts", "shard"), None),
            P(("cuts", "shard"), None),
            P(("cuts", "shard"), None),
        ),
        out_specs=(
            P("cuts", "shard"),
            P(("cuts", "shard"), None),
            P(("cuts", "shard"), None),
            P(("cuts", "shard"), None),
        ),
        check_vma=False,
    )
```
